256 devices in a mesh: batch: 2 (over core), gr: 16 (over z, y_lo), gc: 8 (over x, y_hi).
Axes of the slice: x: 4, y: 4 (y_hi: 2, y_lo: 2; y = y_hi * 2 + y_lo), z: 8, core: 2. Of those that a mesh axis runs over, the one named last changes fastest.
Arguments:
- tokens: bfloat16 [1024, 8192], P(('batch', 'gc'), 'gr'), parts along dimension 0, may hold values from -6 to 6
- gate_weight: bfloat16 [8192, 28672], P('gr', 'gc'), may hold values from -0.0625 to 0.0625
- up_weight: bfloat16 [8192, 28672], P('gr', 'gc'), may hold values from -0.0625 to 0.0625
- down_weight: bfloat16 [28672, 8192], P('gc', 'gr'), may hold values from -0.0625 to 0.0625
- gate_mask: int32 [128, 448], P('gr', 'gc'), may hold values from 0 to 1, as said below
- up_mask: int32 [128, 448], P('gr', 'gc'), may hold values from 0 to 1, as said below
- down_mask: int32 [448, 128], P('gc', 'gr'), may hold values from 0 to 1, as said below
Outputs:
- output: bfloat16 [1024, 8192], P(('batch', 'gc'), 'gr'), parts along dimension 0
The draws below stay inside these ranges and needn't reach their ends.
There are 2 independent parts, one for each index of `batch`. The reference program is written for one: setup_inputs(seed, part) draws one part's arguments, and reference() takes and returns one part's arrays. A program takes and returns all parts, laid end to end along the dimension named above; an argument that names none is the same for every part. Nothing has to cross between parts.
Inputs may be any that keep to these rules, and one draw needn't show every extreme that they name: `gate_mask`: 1 keeps a 64 x 64 block of the projection, 0 prunes it; the share kept differs from one region of the matrix to another. `up_mask`: 1 keeps a 64 x 64 block of the projection, 0 prunes it; the share kept differs from one region of the matrix to another. `down_mask`: 1 keeps a 64 x 64 block of the projection, 0 prunes it; the share kept differs from one region of the matrix to another.
All inputs are finite; a program needn't handle non-finite values.
Results may differ from the reference program's by a relative error of at most 0.022.
Values may be sent and summed in bfloat16 or wider, within the bound.
No kernel may reach another device: no remote copies, remote signals or barrier semaphores. Data moves between devices by JAX's collectives and lax.ppermute only.
A program may use at most 128 MiB of HBM per device.

```python
import jax
import jax.numpy as jnp
from jax import lax

D = 8192
FF = 28672
ROWS = 512
KD = 128
KF = 448
GRID_ROWS = 16
GRID_COLS = 8


def tile_mask(key, count_rows, count_cols, tiles_rows, tiles_cols):
    level_key, block_key = jax.random.split(key)
    levels = jax.random.randint(level_key, (tiles_rows, tiles_cols), 1, 8)
    spread = jnp.repeat(jnp.repeat(levels, count_rows // tiles_rows, axis=0), count_cols // tiles_cols, axis=1)
    block_draw = jax.random.randint(block_key, (count_rows, count_cols), 0, 8)
    return (block_draw < spread).astype(jnp.int32)


def draw_gate_mask(key, part):
    return tile_mask(jax.random.fold_in(key, 11), KD, KF, GRID_ROWS, GRID_COLS)


def draw_up_mask(key, part):
    return tile_mask(jax.random.fold_in(key, 23), KD, KF, GRID_ROWS, GRID_COLS)


def draw_down_mask(key, part):
    return tile_mask(jax.random.fold_in(key, 37), KF, KD, GRID_COLS, GRID_ROWS)


def block_levels(key, extent, pieces, least, largest):
    def one(position, shards_of):
        heights = jax.random.uniform(jax.random.fold_in(jax.random.fold_in(key, 6), position), (shards_of,), jnp.float32, least / len(pieces), largest / len(pieces))
        return jnp.repeat(jnp.exp(heights), extent[position] // shards_of).reshape((-1,) + (1,) * (len(extent) - position - 1))

    loudness = one(*pieces[0])
    for cut in pieces[1:]:
        loudness = loudness * one(*cut)
    return loudness


def bell_draw(stream_key, shape, scale, limit, cuts=(), kind=jnp.bfloat16):
    array = scale * jax.random.normal(stream_key, shape, jnp.float32)
    if cuts:
        array = array * block_levels(stream_key, shape, cuts, -0.22, 0.18)
    return jnp.clip(array, -limit, limit).astype(kind)


def setup_inputs(seed: int = 0, part: int = 0) -> dict:
    streams_of = jax.random.split(jax.random.key(seed), 8)
    own_keys = jax.random.split(jax.random.fold_in(streams_of[7], part), 8)
    return {
        "tokens": bell_draw(own_keys[0], (ROWS, D), 1.0, 6.0, ((0, 8), (1, 16))),
        "gate_weight": bell_draw(streams_of[1], (D, FF), D ** -0.5, 0.0625, ((0, 16), (1, 8))),
        "up_weight": bell_draw(streams_of[2], (D, FF), D ** -0.5, 0.0625, ((0, 16), (1, 8))),
        "down_weight": bell_draw(streams_of[3], (FF, D), (FF // 4) ** -0.5, 0.0625, ((0, 8), (1, 16))),
        "gate_mask": draw_gate_mask(jax.random.fold_in(streams_of[7], 71), part),
        "up_mask": draw_up_mask(jax.random.fold_in(streams_of[7], 71), part),
        "down_mask": draw_down_mask(jax.random.fold_in(streams_of[7], 71), part),
    }


def expand(weight, block_mask):
    count_r, count_c = block_mask.shape
    side_r = weight.shape[0] // count_r
    side_c = weight.shape[1] // count_c
    shaped = weight.reshape(count_r, side_r, count_c, side_c)
    kept = shaped * block_mask[:, None, :, None].astype(weight.dtype)
    return kept.reshape(weight.shape)


def reference(tokens, gate_weight, up_weight, down_weight, gate_mask, up_mask, down_mask):
    gate_kept = expand(gate_weight, gate_mask)
    up_kept = expand(up_weight, up_mask)
    down_kept = expand(down_weight, down_mask)
    group_size = D // GRID_ROWS

    def add_group(shard_index, carry):
        gate_sum, up_sum = carry
        offset = (shard_index * group_size).astype(jnp.int32)
        columns = lax.dynamic_slice_in_dim(tokens, offset, group_size, 1)
        gate_rows = lax.dynamic_slice_in_dim(gate_kept, offset, group_size, 0)
        up_rows = lax.dynamic_slice_in_dim(up_kept, offset, group_size, 0)
        gate_part = jnp.dot(columns, gate_rows, preferred_element_type=jnp.float32).astype(jnp.bfloat16)
        up_part = jnp.dot(columns, up_rows, preferred_element_type=jnp.float32).astype(jnp.bfloat16)
        gate_part, up_part = lax.optimization_barrier((gate_part, up_part))
        return (gate_sum + gate_part.astype(jnp.float32), up_sum + up_part.astype(jnp.float32))

    empty = jnp.zeros((tokens.shape[0], FF), jnp.float32)
    gate_total, up_total = lax.fori_loop(0, GRID_ROWS, add_group, (empty, empty))
    hidden = (jax.nn.silu(gate_total) * up_total).astype(jnp.bfloat16)
    branch = jnp.dot(hidden, down_kept, preferred_element_type=jnp.float32)
    return (tokens.astype(jnp.float32) + branch).astype(jnp.bfloat16)
```

```python
import jax
import jax.numpy as jnp
from jax import lax
from jax.sharding import Mesh, PartitionSpec as P

F32, BF16 = jnp.float32, jnp.bfloat16
SLICES = (896, 896)


def widen(block_mask, side):
    count = block_mask.shape[1]
    spread = (jnp.arange(count * side)[None, :] // side == jnp.arange(count)[:, None]).astype(BF16)
    return jnp.dot(block_mask.astype(BF16), spread, preferred_element_type=F32).astype(BF16)


def keep(weight, wide, row, col, height, width):
    part = lax.dynamic_slice(weight, (row, col), (height, width))
    mask = lax.dynamic_slice(wide, (row // 64, col), (height // 64, width))
    return (part.reshape(height // 64, 64, width) * mask[:, None, :]).reshape(height, width)


def dot(a, b):
    return jnp.dot(a, b, preferred_element_type=F32)


def make(nz, gc):
    up_z = [(i, (i + 1) % nz) for i in range(nz)]
    down_z = [(i, (i - 1) % nz) for i in range(nz)]
    swap = [(0, 1), (1, 0)]

    def both_ways(right, left):
        right, left = lax.optimization_barrier((right, left))
        return lax.optimization_barrier(
            (lax.ppermute(right, "z", up_z), lax.ppermute(left, "z", down_z))
        )

    def on_device(tokens, gate_weight, up_weight, down_weight, gate_mask, up_mask, down_mask):
        rows, depth = tokens.shape
        half = rows // 2
        ff = gate_weight.shape[1] // 2
        core, z, y = lax.axis_index("batch"), lax.axis_index("z"), lax.axis_index("y")
        gate_wide, up_wide = widen(gate_mask, 64), widen(up_mask, 64)
        down_wide = widen(down_mask, 64)

        def pair(row, col, height, width):
            return jnp.concatenate(
                (
                    keep(gate_weight, gate_wide, row, col, height, width),
                    keep(up_weight, up_wide, row, col, height, width),
                ),
                axis=1,
            )

        def across(value):
            near = lax.ppermute(value, "y", swap)
            return near, lax.ppermute(near, "batch", swap)

        starts = [sum(SLICES[:s]) for s in range(len(SLICES))]
        inbound = [
            across(pair(core * (depth // 2), (1 - y) * ff + at, depth // 2, n))
            for at, n in zip(starts, SLICES)
        ]
        down_in = across(
            keep(down_weight, down_wide, (1 - y) * ff + core * (ff // 2), 0, ff // 2, depth)
        )

        spread = jnp.broadcast_to(tokens[None], (2 * gc, rows, depth))
        every = lax.all_to_all(spread, ("y", "gc"), 0, 0, tiled=False)
        every = every.reshape(2, gc * rows, depth)
        double = jnp.concatenate((every, every), axis=1)
        own = lax.dynamic_slice(double, (y, z * rows, 0), (1, gc * rows, depth))[0]
        far_near = lax.dynamic_slice(
            double, (1 - y, z * rows, core * (depth // 2)), (1, gc * rows, depth // 2)
        )[0]
        far_far = lax.dynamic_slice(
            double, (1 - y, z * rows, (1 - core) * (depth // 2)), (1, gc * rows, depth // 2)
        )[0]

        def reduce(part):
            def block(d):
                return part[(d % nz) * rows : (d % nz + 1) * rows].astype(F32)

            far = part[4 * rows : 5 * rows]
            right, left = both_ways(far[:half], far[half:])
            b, c = block(3), block(-3)
            right, left = both_ways(
                jnp.concatenate((b[:half] + right.astype(F32), b[half:]), axis=0).astype(BF16),
                jnp.concatenate((c[:half], c[half:] + left.astype(F32)), axis=0).astype(BF16),
            )
            for d in (2, 1):
                right, left = both_ways(
                    (block(d) + right.astype(F32)).astype(BF16),
                    (block(-d) + left.astype(F32)).astype(BF16),
                )
            return block(0) + right.astype(F32) + left.astype(F32)

        def gather(hidden):
            chunks = [hidden] + [None] * (nz - 1)
            right = left = hidden
            for d in (1, 2, 3):
                right, left = both_ways(right, left)
                chunks[-d % nz], chunks[d] = right, left
            chunks[4] = jnp.concatenate(both_ways(right[:half], left[half:]), axis=0)
            return jnp.concatenate(chunks, axis=0)

        branch_own = branch_far = 0.0
        for at, n, (near, far) in zip(starts, SLICES, inbound):
            kept = pair(0, y * ff + at, depth, n)
            part = (dot(own, kept) + dot(far_near, near) + dot(far_far, far)).astype(BF16)
            total = reduce(part)
            hidden = gather((jax.nn.silu(total[:, :n]) * total[:, n:]).astype(BF16))
            branch_own += dot(hidden, keep(down_weight, down_wide, y * ff + at, 0, n, depth))
            down_far = lax.dynamic_slice(
                jnp.concatenate((*down_in, down_in[0]), axis=0),
                (core * (ff // 2) + at, 0),
                (n, depth),
            )
            branch_far += dot(hidden, down_far)

        def ordered(branch):
            blocks = branch.astype(BF16).reshape(gc, rows, depth)
            return lax.dynamic_slice_in_dim(
                jnp.concatenate((blocks, blocks), axis=0), (nz - z) % nz, gc, 0
            )

        a, b = ordered(branch_own), ordered(branch_far)
        first = y == 0
        leaving = jnp.concatenate((jnp.where(first, a, b), jnp.where(first, b, a)), axis=0)
        arrived = lax.all_to_all(leaving, ("y", "gc"), 0, 0, tiled=False)
        return (tokens.astype(F32) + jnp.sum(arrived.astype(F32), axis=0)).astype(BF16)

    return on_device


def solution(mesh):
    batch, gr, gc = (mesh.shape[a] for a in ("batch", "gr", "gc"))
    fine = Mesh(mesh.devices.reshape(batch, gr // 2, 2, gc), ("batch", "z", "y", "gc"))
    wide, tall = P(("z", "y"), "gc"), P("gc", ("z", "y"))
    rows = P(("batch", "gc"), ("z", "y"))
    return jax.shard_map(
        make(gr // 2, gc),
        mesh=fine,
        in_specs=(rows, wide, wide, tall, wide, wide, tall),
        out_specs=rows,
        check_vma=False,
    )
```

```python
import functools

import jax
import jax.numpy as jnp
from jax import lax
from jax.experimental import pallas as pl
from jax.experimental.pallas import tpu as pltpu
from jax.sharding import Mesh, PartitionSpec as P

F32, BF16 = jnp.float32, jnp.bfloat16
SLICES = (896, 896)


def widen(block_mask, side):
    count = block_mask.shape[1]
    spread = (jnp.arange(count * side)[None, :] // side == jnp.arange(count)[:, None]).astype(BF16)
    return jnp.dot(block_mask.astype(BF16), spread, preferred_element_type=F32).astype(BF16)


def keep(weight, wide, row, col, height, width):
    part = lax.dynamic_slice(weight, (row, col), (height, width))
    mask = lax.dynamic_slice(wide, (row // 64, col), (height // 64, width))
    return (part.reshape(height // 64, 64, width) * mask[:, None, :]).reshape(height, width)


def dot(a, b):
    return jnp.dot(a, b, preferred_element_type=F32)


def after(value, *others):
    return lax.optimization_barrier((value, *others))[0]


def down_kernel(nz, slices, place_ref, *refs):
    *chunk_refs, own_ref, near_ref, far_ref, out_ref, hidden, weight = refs
    core, z, y = place_ref[0], place_ref[1], place_ref[2]
    rows, cols = out_ref.shape[1], out_ref.shape[2]
    at = 0
    per = len(chunk_refs) // len(slices)
    for s, n in enumerate(slices):
        top = 0
        for ref in chunk_refs[s * per : (s + 1) * per]:
            hidden[top : top + ref.shape[0], at : at + n] = ref[...]
            top += ref.shape[0]
        at += n
    part = near_ref.shape[0]
    weight[:, :cols] = own_ref[...]
    weight[pl.ds(pl.multiple_of(core * part, 128), part), cols:] = near_ref[...]
    weight[pl.ds(pl.multiple_of((1 - core) * part, 128), part), cols:] = far_ref[...]
    tile = 256
    for t in range(2 * cols // tile):
        value = jnp.dot(
            hidden[...], weight[:, t * tile : (t + 1) * tile], preferred_element_type=F32
        ).astype(BF16)
        whose, left = divmod(t * tile, cols)
        side = y if whose == 0 else 1 - y
        for j in range(nz):
            out_ref[side * nz + lax.rem(z + j, nz), :, left : left + tile] = value[
                j * rows : (j + 1) * rows
            ]


def down(place, chunks, own, near, far, nz, slices, rows):
    ff, cols = own.shape
    whole = pl.BlockSpec(memory_space=pltpu.VMEM)
    count = len(chunks) + 3
    return pl.pallas_call(
        functools.partial(down_kernel, nz, slices),
        out_shape=jax.ShapeDtypeStruct((2 * nz, rows, cols), BF16),
        in_specs=[pl.BlockSpec(memory_space=pltpu.SMEM)] + [whole] * count,
        out_specs=whole,
        scratch_shapes=[pltpu.VMEM((nz * rows, ff), BF16), pltpu.VMEM((ff, 2 * cols), BF16)],
        compiler_params=pltpu.CompilerParams(vmem_limit_bytes=40 * 1024 * 1024),
        cost_estimate=pl.CostEstimate(
            flops=4 * nz * rows * ff * cols, bytes_accessed=8 * ff * cols, transcendentals=0
        ),
    )(place, *chunks, own, near, far)


def make(nz, gc):
    up_z = [(i, (i + 1) % nz) for i in range(nz)]
    down_z = [(i, (i - 1) % nz) for i in range(nz)]
    swap = [(0, 1), (1, 0)]

    def both_ways(right, left):
        right, left = lax.optimization_barrier((right, left))
        return lax.optimization_barrier(
            (lax.ppermute(right, "z", up_z), lax.ppermute(left, "z", down_z))
        )

    def on_device(tokens, gate_weight, up_weight, down_weight, gate_mask, up_mask, down_mask):
        rows, depth = tokens.shape
        half = rows // 2
        ff = gate_weight.shape[1] // 2
        core, z, y = lax.axis_index("batch"), lax.axis_index("z"), lax.axis_index("y")
        gate_wide, up_wide = widen(gate_mask, 64), widen(up_mask, 64)

        def pair(row, col, height, width):
            return jnp.concatenate(
                (
                    keep(gate_weight, gate_wide, row, col, height, width),
                    keep(up_weight, up_wide, row, col, height, width),
                ),
                axis=1,
            )

        def across(value):
            return lax.ppermute(value, "y", swap)

        def both_cores(near):
            return near, lax.ppermute(near, "batch", swap)

        line = lax.all_to_all(
            jnp.broadcast_to(tokens[None], (4, rows, depth)), ("y", "far"), 0, 0, tiled=False
        )
        starts = [sum(SLICES[:s]) for s in range(len(SLICES))]
        inbound = across(
            after(
                jnp.concatenate(
                    [
                        pair(core * (depth // 2), (1 - y) * ff + at, depth // 2, n)
                        for at, n in zip(starts, SLICES)
                    ],
                    axis=1,
                ),
                line,
            )
        )

        plane = lax.all_to_all(
            jnp.broadcast_to(line[None], (gc // 2, 4, rows, depth)), "x", 0, 0, tiled=False
        )
        every = plane.reshape(gc // 2, 2, 2, rows, depth).swapaxes(0, 1)
        every = every.reshape(2, gc * rows, depth)
        double = jnp.concatenate((every, every), axis=1)
        own = lax.dynamic_slice(double, (y, z * rows, 0), (1, gc * rows, depth))[0]
        far_near = lax.dynamic_slice(
            double, (1 - y, z * rows, core * (depth // 2)), (1, gc * rows, depth // 2)
        )[0]
        far_far = lax.dynamic_slice(
            double, (1 - y, z * rows, (1 - core) * (depth // 2)), (1, gc * rows, depth // 2)
        )[0]

        def reduce(part, steps):
            def block(d):
                return part[(d % nz) * rows : (d % nz + 1) * rows].astype(F32)

            far = part[4 * rows : 5 * rows]
            right, left = both_ways(far[:half], far[half:])
            steps.append(right)
            b, c = block(3), block(-3)
            right, left = both_ways(
                jnp.concatenate((b[:half] + right.astype(F32), b[half:]), axis=0).astype(BF16),
                jnp.concatenate((c[:half], c[half:] + left.astype(F32)), axis=0).astype(BF16),
            )
            steps.append(right)
            for d in (2, 1):
                right, left = both_ways(
                    (block(d) + right.astype(F32)).astype(BF16),
                    (block(-d) + left.astype(F32)).astype(BF16),
                )
                steps.append(right)
            return block(0) + right.astype(F32) + left.astype(F32)

        def gather(hidden):
            chunks = [hidden] + [None] * (nz - 1)
            right = left = hidden
            for d in (1, 2, 3):
                right, left = both_ways(right, left)
                chunks[-d % nz], chunks[d] = right, left
            chunks[4:5] = both_ways(right[:half], left[half:])
            return chunks

        nears = [dot(own, pair(0, y * ff + at, depth, n)) for at, n in zip(starts, SLICES)]
        inbound, *nears = lax.optimization_barrier((inbound, *nears))
        crossed = lax.ppermute(inbound, "batch", swap)
        steps, hiddens = [], []
        for s, (at, n) in enumerate(zip(starts, SLICES)):
            near, far = (side[:, 2 * at : 2 * (at + n)] for side in (inbound, crossed))
            part = (nears[s] + dot(far_near, near) + dot(far_far, far)).astype(BF16)
            steps = []
            total = reduce(part, steps)
            if s == 0:
                down_wide = widen(after(down_mask, steps[0]), 64)
                down_in = across(
                    keep(down_weight, down_wide, (1 - y) * ff + core * (ff // 2), 0, ff // 2, depth)
                )
            hiddens.append((jax.nn.silu(total[:, :n]) * total[:, n:]).astype(BF16))
        near, far = both_cores(after(down_in, steps[2]))
        place = jnp.stack((core, z, y)).astype(jnp.int32)
        own_down = keep(down_weight, down_wide, y * ff, 0, ff, depth)
        chunks = sum((list(gather(hidden)) for hidden in hiddens), [])
        leaving = down(place, chunks, own_down, near, far, nz, SLICES, rows)
        arrived = lax.all_to_all(leaving, ("y", "x", "far"), 0, 0, tiled=False)
        return (tokens.astype(F32) + jnp.sum(arrived.astype(F32), axis=0)).astype(BF16)

    return on_device


def solution(mesh):
    batch, gr, gc = (mesh.shape[a] for a in ("batch", "gr", "gc"))
    fine = Mesh(mesh.devices.reshape(batch, gr // 2, 2, gc // 2, 2), ("batch", "z", "y", "x", "far"))
    wide, tall = P(("z", "y"), ("x", "far")), P(("x", "far"), ("z", "y"))
    rows = P(("batch", "x", "far"), ("z", "y"))
    return jax.shard_map(
        make(gr // 2, gc),
        mesh=fine,
        in_specs=(rows, wide, wide, tall, wide, wide, tall),
        out_specs=rows,
        check_vma=False,
    )
```

```python
import functools

import jax
import jax.numpy as jnp
from jax import lax
from jax.experimental import pallas as pl
from jax.experimental.pallas import tpu as pltpu
from jax.sharding import Mesh, PartitionSpec as P

F32, BF16 = jnp.float32, jnp.bfloat16
SLICES = (896, 896)


def widen(block_mask, side):
    count = block_mask.shape[1]
    spread = (jnp.arange(count * side)[None, :] // side == jnp.arange(count)[:, None]).astype(BF16)
    return jnp.dot(block_mask.astype(BF16), spread, preferred_element_type=F32).astype(BF16)


def keep(weight, wide, row, col, height, width):
    part = lax.dynamic_slice(weight, (row, col), (height, width))
    mask = lax.dynamic_slice(wide, (row // 64, col), (height // 64, width))
    return (part.reshape(height // 64, 64, width) * mask[:, None, :]).reshape(height, width)


def dot(a, b):
    return jnp.dot(a, b, preferred_element_type=F32)


def after(value, *others):
    return lax.optimization_barrier((value, *others))[0]


def down_kernel(nz, slices, place_ref, *refs):
    *chunk_refs, own_ref, near_ref, far_ref, out_ref, hidden, weight = refs
    core, z, y = place_ref[0], place_ref[1], place_ref[2]
    rows, cols = out_ref.shape[1], out_ref.shape[2]
    at = 0
    per = len(chunk_refs) // len(slices)
    for s, n in enumerate(slices):
        top = 0
        for ref in chunk_refs[s * per : (s + 1) * per]:
            hidden[top : top + ref.shape[0], at : at + n] = ref[...]
            top += ref.shape[0]
        at += n
    part = near_ref.shape[0]
    weight[:, :cols] = own_ref[...]
    weight[pl.ds(pl.multiple_of(core * part, 128), part), cols:] = near_ref[...]
    weight[pl.ds(pl.multiple_of((1 - core) * part, 128), part), cols:] = far_ref[...]
    tile = 256
    for t in range(2 * cols // tile):
        value = jnp.dot(
            hidden[...], weight[:, t * tile : (t + 1) * tile], preferred_element_type=F32
        ).astype(BF16)
        whose, left = divmod(t * tile, cols)
        side = y if whose == 0 else 1 - y
        for j in range(nz):
            out_ref[side * nz + lax.rem(z + j, nz), :, left : left + tile] = value[
                j * rows : (j + 1) * rows
            ]


def down(place, chunks, own, near, far, nz, slices, rows):
    ff, cols = own.shape
    whole = pl.BlockSpec(memory_space=pltpu.VMEM)
    count = len(chunks) + 3
    return pl.pallas_call(
        functools.partial(down_kernel, nz, slices),
        out_shape=jax.ShapeDtypeStruct((2 * nz, rows, cols), BF16),
        in_specs=[pl.BlockSpec(memory_space=pltpu.SMEM)] + [whole] * count,
        out_specs=whole,
        scratch_shapes=[pltpu.VMEM((nz * rows, ff), BF16), pltpu.VMEM((ff, 2 * cols), BF16)],
        compiler_params=pltpu.CompilerParams(vmem_limit_bytes=40 * 1024 * 1024),
        cost_estimate=pl.CostEstimate(
            flops=4 * nz * rows * ff * cols, bytes_accessed=8 * ff * cols, transcendentals=0
        ),
    )(place, *chunks, own, near, far)


def make(nz, gc):
    up_z = [(i, (i + 1) % nz) for i in range(nz)]
    down_z = [(i, (i - 1) % nz) for i in range(nz)]
    swap = [(0, 1), (1, 0)]

    def both_ways(right, left):
        right, left = lax.optimization_barrier((right, left))
        return lax.optimization_barrier(
            (lax.ppermute(right, "z", up_z), lax.ppermute(left, "z", down_z))
        )

    def on_device(tokens, gate_weight, up_weight, down_weight, gate_mask, up_mask, down_mask):
        rows, depth = tokens.shape
        half = rows // 2
        ff = gate_weight.shape[1] // 2
        core, z, y = lax.axis_index("batch"), lax.axis_index("z"), lax.axis_index("y")
        gate_wide, up_wide = widen(gate_mask, 64), widen(up_mask, 64)

        def pair(row, col, height, width):
            return [
                keep(gate_weight, gate_wide, row, col, height, width),
                keep(up_weight, up_wide, row, col, height, width),
            ]

        def across(value):
            return lax.ppermute(value, "y", swap)

        def both_cores(near):
            return near, lax.ppermute(near, "batch", swap)

        line = lax.all_to_all(
            jnp.broadcast_to(tokens[None], (4, rows, depth)), ("y", "far"), 0, 0, tiled=False
        )
        starts = [sum(SLICES[:s]) for s in range(len(SLICES))]
        outbound = [
            jnp.concatenate(pair(core * (depth // 2), (1 - y) * ff + at, depth // 2, n), axis=1)
            for at, n in zip(starts, SLICES)
        ]
        outbound = lax.optimization_barrier((*outbound, line))[:-1]
        inbound = [across(value) for value in outbound]
        plane = lax.all_to_all(
            jnp.broadcast_to(line[None], (gc // 2, 4, rows, depth)), "x", 0, 0, tiled=False
        )
        every = plane.reshape(gc // 2, 2, 2, rows, depth).swapaxes(0, 1)
        every = every.reshape(2, gc * rows, depth)
        double = jnp.concatenate((every, every), axis=1)
        own = lax.dynamic_slice(double, (y, z * rows, 0), (1, gc * rows, depth))[0]
        far_near = lax.dynamic_slice(
            double, (1 - y, z * rows, core * (depth // 2)), (1, gc * rows, depth // 2)
        )[0]
        far_far = lax.dynamic_slice(
            double, (1 - y, z * rows, (1 - core) * (depth // 2)), (1, gc * rows, depth // 2)
        )[0]

        def reduce(part, steps, need=None, use=None):
            def block(d):
                return part[(d % nz) * rows : (d % nz + 1) * rows].astype(F32)

            far = part[4 * rows : 5 * rows]
            right, left = both_ways(far[:half], far[half:])
            steps.append(right)
            if need is not None:
                right, left, need = lax.optimization_barrier((right, left, need))
            b, c = block(3), block(-3)
            right, left = both_ways(
                jnp.concatenate((b[:half] + right.astype(F32), b[half:]), axis=0).astype(BF16),
                jnp.concatenate((c[:half], c[half:] + left.astype(F32)), axis=0).astype(BF16),
            )
            steps.append(right)
            if need is not None:
                right, left, need = lax.optimization_barrier((right, left, use(need)))
            for d in (2, 1):
                right, left = both_ways(
                    (block(d) + right.astype(F32)).astype(BF16),
                    (block(-d) + left.astype(F32)).astype(BF16),
                )
                steps.append(right)
            return block(0) + right.astype(F32) + left.astype(F32), need

        def gather(hidden):
            chunks = [hidden] + [None] * (nz - 1)
            right = left = hidden
            for d in (1, 2, 3):
                right, left = both_ways(right, left)
                chunks[-d % nz], chunks[d] = right, left
            chunks[4:5] = both_ways(right[:half], left[half:])
            return chunks

        nears = [dot(own, jnp.concatenate(pair(0, y * ff + at, depth, n), axis=1)) for at, n in zip(starts, SLICES)]
        inbound[0], *nears = lax.optimization_barrier((inbound[0], *nears))
        steps, hiddens = [], []
        def product(s, arriving):
            near, far = both_cores(arriving)
            return (nears[s] + dot(far_near, near) + dot(far_far, far)).astype(BF16)

        part = product(0, inbound[0])
        for s, n in enumerate(SLICES):
            steps = []
            if s == 0:
                total, part = reduce(part, steps, inbound[1], lambda value: product(1, value))
            else:
                total, _ = reduce(part, steps)
            hiddens.append((jax.nn.silu(total[:, :n]) * total[:, n:]).astype(BF16))
            if s == 0:
                down_wide = widen(after(down_mask, steps[1]), 64)
                down_in = across(
                    keep(down_weight, down_wide, (1 - y) * ff + core * (ff // 2), 0, ff // 2, depth)
                )
        near, far = both_cores(after(down_in, steps[2]))
        place = jnp.stack((core, z, y)).astype(jnp.int32)
        own_down = keep(down_weight, down_wide, y * ff, 0, ff, depth)
        chunks = sum((list(gather(hidden)) for hidden in hiddens), [])
        leaving = down(place, chunks, own_down, near, far, nz, SLICES, rows)
        arrived = lax.all_to_all(leaving, ("y", "x", "far"), 0, 0, tiled=False)
        return (tokens.astype(F32) + jnp.sum(arrived.astype(F32), axis=0)).astype(BF16)

    return on_device


def solution(mesh):
    batch, gr, gc = (mesh.shape[a] for a in ("batch", "gr", "gc"))
    fine = Mesh(mesh.devices.reshape(batch, gr // 2, 2, gc // 2, 2), ("batch", "z", "y", "x", "far"))
    wide, tall = P(("z", "y"), ("x", "far")), P(("x", "far"), ("z", "y"))
    rows = P(("batch", "x", "far"), ("z", "y"))
    return jax.shard_map(
        make(gr // 2, gc),
        mesh=fine,
        in_specs=(rows, wide, wide, tall, wide, wide, tall),
        out_specs=rows,
        check_vma=False,
    )
```

```python
import functools

import jax
import jax.numpy as jnp
from jax import lax
from jax.experimental import pallas as pl
from jax.experimental.pallas import tpu as pltpu
from jax.sharding import Mesh, PartitionSpec as P

F32, BF16 = jnp.float32, jnp.bfloat16
SLICES = (896, 896)


def widen(block_mask, side):
    count = block_mask.shape[1]
    spread = (jnp.arange(count * side)[None, :] // side == jnp.arange(count)[:, None]).astype(BF16)
    return jnp.dot(block_mask.astype(BF16), spread, preferred_element_type=F32).astype(BF16)


def keep(weight, wide, row, col, height, width):
    part = lax.dynamic_slice(weight, (row, col), (height, width))
    mask = lax.dynamic_slice(wide, (row // 64, col), (height // 64, width))
    return (part.reshape(height // 64, 64, width) * mask[:, None, :]).reshape(height, width)


def dot(a, b):
    return jnp.dot(a, b, preferred_element_type=F32)


def after(value, *others):
    return lax.optimization_barrier((value, *others))[0]


def down_kernel(nz, slices, place_ref, *refs):
    *chunk_refs, own_ref, near_ref, far_ref, out_ref, hidden, weight = refs
    core, z, y = place_ref[0], place_ref[1], place_ref[2]
    rows, cols = out_ref.shape[1], out_ref.shape[2]
    at = 0
    per = len(chunk_refs) // len(slices)
    for s, n in enumerate(slices):
        top = 0
        for ref in chunk_refs[s * per : (s + 1) * per]:
            hidden[top : top + ref.shape[0], at : at + n] = ref[...]
            top += ref.shape[0]
        at += n
    part = near_ref.shape[0]
    weight[:, :cols] = own_ref[...]
    weight[pl.ds(pl.multiple_of(core * part, 128), part), cols:] = near_ref[...]
    weight[pl.ds(pl.multiple_of((1 - core) * part, 128), part), cols:] = far_ref[...]
    tile = 256
    for t in range(2 * cols // tile):
        value = jnp.dot(
            hidden[...], weight[:, t * tile : (t + 1) * tile], preferred_element_type=F32
        ).astype(BF16)
        whose, left = divmod(t * tile, cols)
        side = y if whose == 0 else 1 - y
        for j in range(nz):
            out_ref[side * nz + lax.rem(z + j, nz), :, left : left + tile] = value[
                j * rows : (j + 1) * rows
            ]


def down(place, chunks, own, near, far, nz, slices, rows):
    ff, cols = own.shape
    whole = pl.BlockSpec(memory_space=pltpu.VMEM)
    count = len(chunks) + 3
    return pl.pallas_call(
        functools.partial(down_kernel, nz, slices),
        out_shape=jax.ShapeDtypeStruct((2 * nz, rows, cols), BF16),
        in_specs=[pl.BlockSpec(memory_space=pltpu.SMEM)] + [whole] * count,
        out_specs=whole,
        scratch_shapes=[pltpu.VMEM((nz * rows, ff), BF16), pltpu.VMEM((ff, 2 * cols), BF16)],
        compiler_params=pltpu.CompilerParams(vmem_limit_bytes=40 * 1024 * 1024),
        cost_estimate=pl.CostEstimate(
            flops=4 * nz * rows * ff * cols, bytes_accessed=8 * ff * cols, transcendentals=0
        ),
    )(place, *chunks, own, near, far)


def make(nz, gc):
    up_z = [(i, (i + 1) % nz) for i in range(nz)]
    down_z = [(i, (i - 1) % nz) for i in range(nz)]
    swap = [(0, 1), (1, 0)]

    def both_ways(right, left):
        right, left = lax.optimization_barrier((right, left))
        return lax.optimization_barrier(
            (lax.ppermute(right, "z", up_z), lax.ppermute(left, "z", down_z))
        )

    def on_device(tokens, gate_weight, up_weight, down_weight, gate_mask, up_mask, down_mask):
        rows, depth = tokens.shape
        half = rows // 2
        ff = gate_weight.shape[1] // 2
        core, z, y = lax.axis_index("batch"), lax.axis_index("z"), lax.axis_index("y")
        gate_wide, up_wide = widen(gate_mask, 64), widen(up_mask, 64)

        def pair(row, col, height, width):
            return jnp.concatenate(
                (
                    keep(gate_weight, gate_wide, row, col, height, width),
                    keep(up_weight, up_wide, row, col, height, width),
                ),
                axis=1,
            )

        def across(value):
            return lax.ppermute(value, "y", swap)

        def both_cores(near):
            return near, lax.ppermute(near, "batch", swap)

        line = lax.all_to_all(
            jnp.broadcast_to(tokens[None], (4, rows, depth)), ("y", "far"), 0, 0, tiled=False
        )
        starts = [sum(SLICES[:s]) for s in range(len(SLICES))]
        inbound = across(
            after(
                jnp.concatenate(
                    [
                        pair(core * (depth // 2), (1 - y) * ff + at, depth // 2, n)
                        for at, n in zip(starts, SLICES)
                    ],
                    axis=1,
                ),
                line,
            )
        )

        plane = lax.all_to_all(
            jnp.broadcast_to(line[None], (gc // 2, 4, rows, depth)), "x", 0, 0, tiled=False
        )
        every = plane.reshape(gc // 2, 2, 2, rows, depth).swapaxes(0, 1)
        every = every.reshape(2, gc * rows, depth)
        double = jnp.concatenate((every, every), axis=1)
        own = lax.dynamic_slice(double, (y, z * rows, 0), (1, gc * rows, depth))[0]
        far_near = lax.dynamic_slice(
            double, (1 - y, z * rows, core * (depth // 2)), (1, gc * rows, depth // 2)
        )[0]
        far_far = lax.dynamic_slice(
            double, (1 - y, z * rows, (1 - core) * (depth // 2)), (1, gc * rows, depth // 2)
        )[0]

        def reduce(part, steps):
            def block(d):
                return part[(d % nz) * rows : (d % nz + 1) * rows].astype(F32)

            far = part[4 * rows : 5 * rows]
            right, left = both_ways(far[:half], far[half:])
            steps.append(right)
            b, c = block(3), block(-3)
            right, left = both_ways(
                jnp.concatenate((b[:half] + right.astype(F32), b[half:]), axis=0).astype(BF16),
                jnp.concatenate((c[:half], c[half:] + left.astype(F32)), axis=0).astype(BF16),
            )
            steps.append(right)
            for d in (2, 1):
                right, left = both_ways(
                    (block(d) + right.astype(F32)).astype(BF16),
                    (block(-d) + left.astype(F32)).astype(BF16),
                )
                steps.append(right)
            return block(0) + right.astype(F32) + left.astype(F32)

        def gather(hidden):
            chunks = [hidden] + [None] * (nz - 1)
            right = left = hidden
            for d in (1, 2, 3):
                right, left = both_ways(right, left)
                chunks[-d % nz], chunks[d] = right, left
            chunks[4:5] = both_ways(right[:half], left[half:])
            return chunks

        nears = [dot(own, pair(0, y * ff + at, depth, n)) for at, n in zip(starts, SLICES)]
        inbound, *nears = lax.optimization_barrier((inbound, *nears))
        crossed = lax.ppermute(inbound, "batch", swap)
        steps, hiddens = [], []
        for s, (at, n) in enumerate(zip(starts, SLICES)):
            near, far = (side[:, 2 * at : 2 * (at + n)] for side in (inbound, crossed))
            part = (nears[s] + dot(far_near, near) + dot(far_far, far)).astype(BF16)
            steps = []
            total = reduce(part, steps)
            if s == 0:
                down_wide = widen(after(down_mask, steps[0]), 64)
                down_in = across(
                    keep(down_weight, down_wide, (1 - y) * ff + core * (ff // 2), 0, ff // 2, depth)
                )
            hiddens.append((jax.nn.silu(total[:, :n]) * total[:, n:]).astype(BF16))
        near, far = both_cores(after(down_in, steps[2]))
        place = jnp.stack((core, z, y)).astype(jnp.int32)
        own_down = keep(down_weight, down_wide, y * ff, 0, ff, depth)
        own_down, hiddens[-1] = lax.optimization_barrier((own_down, hiddens[-1]))
        chunks = sum((list(gather(hidden)) for hidden in hiddens), [])
        leaving = down(place, chunks, own_down, near, far, nz, SLICES, rows)
        arrived = lax.all_to_all(leaving, ("y", "x", "far"), 0, 0, tiled=False)
        return (tokens.astype(F32) + jnp.sum(arrived.astype(F32), axis=0)).astype(BF16)

    return on_device


def solution(mesh):
    batch, gr, gc = (mesh.shape[a] for a in ("batch", "gr", "gc"))
    fine = Mesh(mesh.devices.reshape(batch, gr // 2, 2, gc // 2, 2), ("batch", "z", "y", "x", "far"))
    wide, tall = P(("z", "y"), ("x", "far")), P(("x", "far"), ("z", "y"))
    rows = P(("batch", "x", "far"), ("z", "y"))
    return jax.shard_map(
        make(gr // 2, gc),
        mesh=fine,
        in_specs=(rows, wide, wide, tall, wide, wide, tall),
        out_specs=rows,
        check_vma=False,
    )
```
